32 devices in a mesh: grp: 2 (over x), comp: 8 (over z, y), lon: 2 (over core).
Axes of the slice: x: 2, y: 2, z: 4, core: 2. Of those that a mesh axis runs over, the one named last changes fastest.
Arguments:
- spectrum: float32 [2304, 48, 256], P(('grp', 'comp'), None, 'lon'), parts along dimension 0, may hold values from 0.05 to 2
- water_depth: float32 [48, 256], P(None, 'lon'), may hold values from 5 to 5000
- sea_mask: int32 [48, 256], P(None, 'lon'), may hold values 0 or 1
- wind_field: float32 [2, 96, 256], P(None, 'grp', 'lon'), parts along dimension 1, may hold values from -8 to 8
- slot_comp: int32 [1152], replicated, may hold values from 0 to 1151, as said below
- substeps: int32 [32], replicated, may hold values from 1 to 4
- coupling: bfloat16 [5, 36, 36], replicated, may hold values from -0.4375 to 0.4375
Outputs:
- spectrum_new: float32 [2304, 48, 256], P(('grp', 'comp'), None, 'lon'), parts along dimension 0
The draws below stay inside these ranges and needn't reach their ends.
There are 2 independent parts, one for each index of `grp`. The reference program is written for one: setup_inputs(seed, part) draws one part's arguments, and reference() takes and returns one part's arrays. A program takes and returns all parts, laid end to end along the dimension named above; an argument that names none is the same for every part. Nothing has to cross between parts.
Inputs may be any that keep to these rules, and one draw needn't show every extreme that they name: A permutation: slot s holds component slot_comp[s], components numbered k = f * 36 + d; slots are ordered by frequency up to a shift: slot_comp[s] // 36 differs from 32 s / 1152 by at most 3.
All inputs are finite; a program needn't handle non-finite values. No bound on the sum of `sea_mask` on one device may be relied on, other than what follows from the above.
Results may differ from the reference program's by a relative error of at most 0.015.
Values may be sent and summed in bfloat16 or wider, within the bound.
A program may use at most 128 MiB of HBM per device.

```python
import math
import jax
import jax.numpy as jnp
from jax import lax

NDIR = 36
NFREQ = 32
NLAT = 48
SLOTS = 1152
NLON = 256


def draw_substeps(key, part):
    index = jnp.arange(NFREQ, dtype=jnp.int32)
    base = 4 - 4 * index // NFREQ
    jitter = jax.random.randint(key, (NFREQ,), -1, 2)
    counts = jnp.clip(base + jitter, 1, 4)
    counts = counts.at[0].set(4)
    counts = counts.at[NFREQ - 1].set(1)
    return counts.astype(jnp.int32)


def draw_slot_comp(key, part):
    count_all = NDIR * NFREQ
    component = jnp.arange(count_all, dtype=jnp.int32)
    jitter = jax.random.randint(jax.random.fold_in(key, 11), (count_all,), 0, 12)
    shuffled = jax.random.permutation(jax.random.fold_in(key, 12), count_all).astype(jnp.int32)
    score = (component // NDIR * 4 + jitter) * count_all + shuffled
    return jnp.argsort(score).astype(jnp.int32)


def set_ends(drawn, key, smallest, largest):
    shape = drawn.shape
    place = [jax.random.randint(jax.random.fold_in(key, axis), (), 0, shape[axis]) for axis in range(len(shape))]
    drawn = drawn.at[tuple(place)].set(smallest)
    longest = shape.index(max(shape))
    place[longest] = (place[longest] + 1) % shape[longest]
    return drawn.at[tuple(place)].set(largest)


def level_of(rng, shape, split, smallest, high):
    gain = 1.0
    for position, parts in split:
        steps = jax.random.uniform(jax.random.fold_in(jax.random.fold_in(rng, 6), position), (parts,), jnp.float32, smallest / len(split), high / len(split))
        gain = gain * jnp.repeat(jnp.exp(steps), shape[position] // parts).reshape((-1,) + (1,) * (len(shape) - 1 - position))
    return gain


def scatter_about(key, dims, spread, limit, split=(), kind=jnp.bfloat16):
    drawn = spread * jax.random.normal(key, dims, jnp.float32)
    if split:
        drawn = drawn * level_of(key, dims, split, -0.22, 0.18)
    return jnp.clip(drawn, -limit, limit).astype(kind)


def setup_inputs(seed: int = 0, part: int = 0) -> dict:
    key_of = jax.random.split(jax.random.key(seed), 8)
    part_keys = jax.random.split(jax.random.fold_in(key_of[7], part), 8)
    spectrum = jnp.clip(jnp.exp(math.log(2.0) - 3.6888794 * jax.random.uniform(part_keys[0], (SLOTS, NLAT, NLON), jnp.float32) ** level_of(part_keys[0], (SLOTS, NLAT, NLON), ((0, 8), (2, 2)), -0.2, 0.2)), 0.05, 2.0)
    water_depth = jnp.clip(jnp.exp(math.log(5000.0) - 6.9077553 * jax.random.uniform(key_of[1], (NLAT, NLON), jnp.float32) ** level_of(key_of[1], (NLAT, NLON), ((1, 2),), -0.2, 0.2)), 5.0, 5000.0)
    sea_mask = set_ends((jax.random.randint(key_of[2], (NLAT, NLON), 0, 10) < 7).astype(jnp.int32), jax.random.fold_in(key_of[2], 1), 0, 1)
    wind_field = scatter_about(part_keys[3], (2, NLAT, NLON), 2.0, 8.0, ((2, 2),), jnp.float32)
    slot_comp = draw_slot_comp(jax.random.fold_in(key_of[7], 71), part)
    substeps = draw_substeps(jax.random.fold_in(key_of[7], 71), part)
    coupling = scatter_about(key_of[6], (5, NDIR, NDIR), (5 * NDIR) ** -0.5, 0.4375)
    return {"spectrum": spectrum, "water_depth": water_depth, "sea_mask": sea_mask, "wind_field": wind_field, "slot_comp": slot_comp, "substeps": substeps, "coupling": coupling}


def take_range(values, low_edge, high_edge, dimension):
    return lax.slice_in_dim(values, low_edge, high_edge, axis=dimension)

def advect(quantity, velocity, ocean_rows, dimension):
    extent = quantity.shape[dimension]
    face_speed = 0.5 * (take_range(velocity, 1, extent - 2, dimension) + take_range(velocity, 2, extent - 1, dimension))
    face_speed = face_speed * take_range(ocean_rows, 1, extent - 2, dimension) * take_range(ocean_rows, 2, extent - 1, dimension)
    behind = take_range(quantity, 0, extent - 3, dimension)
    before = take_range(quantity, 1, extent - 2, dimension)
    after = take_range(quantity, 2, extent - 1, dimension)
    beyond = take_range(quantity, 3, extent, dimension)
    forward = face_speed >= 0.0
    upwind = jnp.where(forward, before, after)
    downwind = jnp.where(forward, after, before)
    farther = jnp.where(forward, behind, beyond)
    courant = jnp.abs(face_speed)
    face_value = 0.5 * (upwind + downwind) - 0.5 * courant * (downwind - upwind) - (1.0 - courant * courant) / 6.0 * (downwind - 2.0 * upwind + farther)
    fluxes = face_speed * face_value
    return take_range(quantity, 2, extent - 2, dimension) - (take_range(fluxes, 1, extent - 3, dimension) - take_range(fluxes, 0, extent - 4, dimension))

def pad_rows(values):
    return jnp.pad(values, ((0, 0), (2, 2), (0, 0)))

def wrap_columns(values):
    return jnp.concatenate([values[:, :, -2:], values, values[:, :, :2]], axis=2)

def banded(coupling, values):
    accumulated = None
    for offset_index in range(5):
        offset = offset_index - 2
        product = jnp.einsum('ij,fjc->fic', coupling[offset_index].astype(jnp.float32), values.astype(jnp.float32))
        padded = jnp.pad(product, ((2, 2), (0, 0), (0, 0)))
        shifted = padded[2 + offset:2 + offset + NFREQ]
        accumulated = shifted if accumulated is None else accumulated + shifted
    return accumulated

def sources(natural, weather, coupling):
    frequency = 0.0418 * jnp.power(1.1, jnp.arange(NFREQ, dtype=jnp.int32).astype(jnp.float32))
    freq_scale = jnp.sqrt(frequency / 0.2)
    heading = 2.0 * math.pi * (jnp.arange(NDIR, dtype=jnp.int32).astype(jnp.float32) + 0.5) / NDIR
    projected = jnp.cos(heading)[:, None] * weather[0][None, :] + jnp.sin(heading)[:, None] * weather[1][None, :]
    growth_rate = 0.3 * jnp.maximum(0.0, freq_scale[:, None, None] * projected[None] - 1.0)
    energy = natural.astype(jnp.float32)
    square = (energy * energy).astype(jnp.bfloat16)
    linear_part = banded(coupling, natural)
    square_part = banded(coupling, square)
    growth = growth_rate * energy
    transfer = 0.5 * (energy * square_part - energy * energy * linear_part)
    return (0.5 * (growth + transfer)).astype(jnp.bfloat16)

def reference(spectrum, water_depth, sea_mask, wind_field, slot_comp, substeps, coupling):
    freq_index = slot_comp // NDIR
    dir_index = slot_comp % NDIR
    ocean = sea_mask.astype(jnp.float32)
    energy = spectrum * ocean[None]
    frequency = 0.0418 * jnp.power(1.1, freq_index.astype(jnp.float32))
    wavenumber = (2.0 * math.pi * frequency) ** 2 / 9.81
    group_speed = 0.8 * jnp.sqrt(jnp.tanh(wavenumber[:, None, None] * water_depth[None])) * ocean[None]
    heading = 2.0 * math.pi * (dir_index.astype(jnp.float32) + 0.5) / NDIR
    east_speed = group_speed * jnp.cos(heading)[:, None, None]
    north_speed = group_speed * jnp.sin(heading)[:, None, None]
    step_count = jnp.take(substeps, freq_index)
    ocean_rows = ocean[None]
    for substep in range(4):
        advanced = advect(wrap_columns(energy), wrap_columns(east_speed), wrap_columns(ocean_rows), 2)
        advanced = advect(pad_rows(advanced), pad_rows(north_speed), pad_rows(ocean_rows), 1)
        active = (step_count > substep)[:, None, None]
        energy = jnp.where(active, advanced, energy)
    cell_count = NLAT * NLON
    flattened = energy.reshape(SLOTS, cell_count)
    inverse = jnp.zeros((SLOTS,), jnp.int32).at[slot_comp].set(jnp.arange(SLOTS, dtype=jnp.int32))
    natural = jnp.take(flattened, inverse, axis=0).astype(jnp.bfloat16).reshape(NFREQ, NDIR, cell_count)
    increment = sources(natural, wind_field.reshape(2, cell_count), coupling).reshape(SLOTS, cell_count)
    returned = jnp.take(increment, slot_comp, axis=0)
    return (flattened + returned.astype(jnp.float32)).reshape(SLOTS, NLAT, NLON)
```

```python
import functools
import math

import jax
import jax.numpy as jnp
from jax import lax
from jax.experimental import pallas as pl
from jax.experimental.pallas import tpu as pltpu
from jax.sharding import PartitionSpec as P

NDIR = 36
NFREQ = 32
ROUND = 16
ROWS = 2
CHUNKS = 2
REACH = 8
NOWHERE = -100000
VMEM = 48 * 1024 * 1024


def round_up(value, step):
    return (value + step - 1) // step * step


def advect_kernel(
    place, steps, mine, other, depth, ocean, face_x, face_y, params, out_mine, out_other,
    q, r, ax, bx, cx, ay, by, cy
):
    lat = depth.shape[0]
    width = depth.shape[2]
    half = width // 2
    wave = params[0][:, :1][None]
    east = params[1][:, :1][None]
    north = params[2][:, :1][None]
    count = params[3][:, :1][None]
    zeros = jnp.zeros((2, ROUND, width), jnp.float32)
    r[0:2] = zeros
    r[lat + 2 : lat + 4] = zeros
    q[:, :, 0:half] = jnp.swapaxes(mine[...], 0, 1)
    q[:, :, half:width] = jnp.swapaxes(other[...].astype(jnp.float32), 0, 1)

    def prepare(i, carry):
        rows = pl.ds(i * ROWS, ROWS)
        sea = ocean[rows]
        r[pl.ds(i * ROWS + 2, ROWS)] = 0.8 * jnp.sqrt(jnp.tanh(wave * depth[rows])) * sea
        q[rows] = q[rows] * sea
        return carry

    lax.fori_loop(0, lat // ROWS, prepare, 0)

    def weights(c):
        first = 0.5 * c * (1.0 + c)
        return first, 0.5 * c * (1.0 - c), first * (1.0 - c) * (1.0 / 3.0)

    def coefficients(i, carry):
        rows = pl.ds(i * ROWS, ROWS)
        speed = r[pl.ds(i * ROWS + 2, ROWS)]
        above = r[pl.ds(i * ROWS + 3, ROWS)]
        ahead = pltpu.roll(speed, width - 1, 2)
        ax[rows], bx[rows], cx[rows] = weights((speed + ahead) * east * face_x[rows])
        ay[rows], by[rows], cy[rows] = weights((speed + above) * north * face_y[rows])
        return carry

    lax.fori_loop(0, lat // ROWS, coefficients, 0)

    def substep(t, carry):
        def along_x(i, inner):
            rows = pl.ds(i * ROWS, ROWS)
            here = q[rows]
            ahead = pltpu.roll(here, width - 1, 2)
            bend = pltpu.roll(here, 1, 2) + ahead - 2.0 * here
            bend_ahead = pltpu.roll(bend, width - 1, 2)
            third = cx[rows]
            flux = (
                ax[rows] * here
                + bx[rows] * ahead
                - third * jnp.where(third >= 0.0, bend, bend_ahead)
            )
            r[pl.ds(i * ROWS + 2, ROWS)] = here - (flux - pltpu.roll(flux, 1, 2))
            return inner

        lax.fori_loop(0, lat // ROWS, along_x, 0)
        active = count > t.astype(jnp.float32)

        def along_y(i, last):
            rows = pl.ds(i * ROWS, ROWS)
            around = r[pl.ds(i * ROWS + 1, ROWS + 3)]
            bend = around[:-2] + around[2:] - 2.0 * around[1:-1]
            here = around[1:-2]
            third = cy[rows]
            flux = (
                ay[rows] * here
                + by[rows] * around[2:-1]
                - third * jnp.where(third >= 0.0, bend[:-1], bend[1:])
            )
            below = jnp.concatenate([last, flux[:-1]], axis=0)
            q[rows] = jnp.where(active, here - (flux - below), q[rows])
            return flux[-1:]

        lax.fori_loop(0, lat // ROWS, along_y, jnp.zeros((1, ROUND, width), jnp.float32))
        return carry

    lax.fori_loop(0, steps[pl.program_id(0)], substep, 0)
    out_mine[...] = q[:, :, 0:half].astype(jnp.bfloat16)
    out_other[...] = q[:, :, half:width].astype(jnp.bfloat16)


def advance(place, steps, mine, other, depth, ocean, face_x, face_y, params):
    handled, lat, half = other.shape
    whole = pl.BlockSpec((lat, 1, 2 * half), lambda i, place, steps: (0, 0, 0))
    field = pltpu.VMEM((lat, ROUND, 2 * half), jnp.float32)
    out = pl.BlockSpec((lat, ROUND, half), lambda i, place, steps: (0, i, 0))
    shape = jax.ShapeDtypeStruct((lat, handled, half), jnp.bfloat16)
    return pl.pallas_call(
        advect_kernel,
        grid_spec=pltpu.PrefetchScalarGridSpec(
            num_scalar_prefetch=2,
            grid=(handled // ROUND,),
            in_specs=[
                pl.BlockSpec((ROUND, lat, half), lambda i, place, steps: (i + place[0], 0, 0)),
                pl.BlockSpec((ROUND, lat, half), lambda i, place, steps: (i, 0, 0)),
                whole,
                whole,
                whole,
                whole,
                pl.BlockSpec((4, ROUND, half), lambda i, place, steps: (0, i, 0)),
            ],
            out_specs=[out, out],
            scratch_shapes=[
                field,
                pltpu.VMEM((lat + 4, ROUND, 2 * half), jnp.float32),
            ]
            + [field] * 6,
        ),
        out_shape=[shape, shape],
        compiler_params=pltpu.CompilerParams(vmem_limit_bytes=VMEM),
        cost_estimate=pl.CostEstimate(
            flops=120 * handled * lat * half * 2,
            bytes_accessed=10 * handled * lat * half * 2,
            transcendentals=0,
        ),
        name="advance",
    )(place, steps, mine, other, depth, ocean, face_x, face_y, params)


def source_kernel(pieces, matrix, scales, wind, *refs):
    inputs, outputs = refs[:pieces], refs[pieces:]
    slots = inputs[0].shape[1]

    def pair(ref):
        return jnp.concatenate([ref[0], ref[1]], axis=1)

    def twice(ref):
        return jnp.concatenate([ref, ref], axis=1)

    near = jnp.concatenate([pair(ref) for ref in inputs], axis=0)
    wide = near.astype(jnp.float32)
    square = (wide * wide).astype(jnp.bfloat16)
    wind_east = jnp.concatenate([wind[0, 0], wind[0, 1]], axis=1)
    wind_north = jnp.concatenate([wind[1, 0], wind[1, 1]], axis=1)
    half = inputs[0].shape[2]
    for part in range(2):
        rows = slice(part * slots, part * slots + slots)
        linear_part = jnp.dot(matrix[rows, :], near, preferred_element_type=jnp.float32)
        square_part = jnp.dot(matrix[rows, :], square, preferred_element_type=jnp.float32)
        energy = wide[rows]
        push = twice(scales[0, rows]) * wind_east + twice(scales[1, rows]) * wind_north
        rate = 0.3 * jnp.maximum(0.0, push - 1.0)
        transfer = 0.5 * (energy * square_part - energy * energy * linear_part)
        change = (0.5 * (rate * energy + transfer)).astype(jnp.bfloat16)
        outputs[part][0] = change[:, :half]
        outputs[part][1] = change[:, half:]


def sources(matrix, scales, wind, inputs):
    rows, slots, half = inputs[0].shape
    block = pl.BlockSpec((2, slots, half), lambda i: (i, 0, 0))
    shape = jax.ShapeDtypeStruct((rows, slots, half), jnp.bfloat16)
    return pl.pallas_call(
        functools.partial(source_kernel, len(inputs)),
        grid=(rows // 2,),
        in_specs=[
            pl.BlockSpec(matrix.shape, lambda i: (0, 0)),
            pl.BlockSpec(scales.shape, lambda i: (0, 0, 0)),
            pl.BlockSpec((2, 2, 1, half), lambda i: (0, i, 0, 0)),
        ]
        + [block] * len(inputs),
        out_specs=[block, block],
        out_shape=[shape, shape],
        compiler_params=pltpu.CompilerParams(vmem_limit_bytes=VMEM),
        cost_estimate=pl.CostEstimate(
            flops=4 * matrix.size * rows * half,
            bytes_accessed=2 * (len(inputs) + 2) * rows * slots * half,
            transcendentals=0,
        ),
        name="sources",
    )(matrix, scales, wind, *inputs)


def finish_kernel(chunks, place, natural, *refs):
    changes, out = refs[: 2 * chunks], refs[2 * chunks]
    part_rows = natural.shape[0] // 2
    chunk_rows = part_rows // chunks
    for which in range(2):
        part = place[1] if which == 0 else 1 - place[1]
        start = pl.multiple_of(part * part_rows, 8)
        change = jnp.concatenate(
            [changes[which * chunks + chunk][...] for chunk in range(chunks)], axis=0
        ).astype(jnp.float32)
        total = natural[pl.ds(start, part_rows)].astype(jnp.float32) + change
        out[:, pl.ds(start, part_rows), :] = jnp.swapaxes(total, 0, 1)


def finish(place, natural, changes):
    lat, slots, half = natural.shape
    blocks = slots // ROUND
    return pl.pallas_call(
        functools.partial(finish_kernel, len(changes) // 2),
        grid_spec=pltpu.PrefetchScalarGridSpec(
            num_scalar_prefetch=1,
            grid=(blocks,),
            in_specs=[pl.BlockSpec((lat, ROUND, half), lambda i, place: (0, i, 0))]
            + [
                pl.BlockSpec((change.shape[0], ROUND, half), lambda i, place: (0, i, 0))
                for change in changes
            ],
            out_specs=pl.BlockSpec(
                (ROUND, lat, half), lambda i, place: (lax.rem(i + place[0], blocks), 0, 0)
            ),
        ),
        out_shape=jax.ShapeDtypeStruct((slots, lat, half), jnp.float32),
        compiler_params=pltpu.CompilerParams(vmem_limit_bytes=VMEM),
        name="finish",
    )(place, natural, *changes)


def frequency_of(index):
    return 0.0418 * jnp.power(1.1, index.astype(jnp.float32))


def heading_of(index):
    return 2.0 * math.pi * (index.astype(jnp.float32) + 0.5) / NDIR


def over_lanes(values, lanes):
    return jnp.broadcast_to(values[:, None], (values.shape[0], lanes))


def on_device(spectrum, water_depth, sea_mask, wind_field, slot_comp, substeps, coupling):
    slots, lat, half = spectrum.shape
    comp_count = lax.axis_size("comp")
    groups = comp_count // 2
    padded = round_up(slots, ROUND)
    handled = round_up(padded // 2, ROUND)
    rest = padded - handled
    comp_place = lax.axis_index("comp")
    lon_place = lax.axis_index("lon")
    member = comp_place % 2
    group = comp_place // 2
    places = 2 * NFREQ // comp_count
    reach = (REACH + places - 1) // places
    swap = [(0, 1), (1, 0)]
    pairs = [(i, i ^ 1) for i in range(comp_count)]

    comps = jnp.pad(
        slot_comp.reshape(comp_count, slots),
        ((0, 0), (0, padded - slots)),
        constant_values=NOWHERE,
    )
    own_start = lon_place * rest
    order = (jnp.arange(padded, dtype=jnp.int32) + own_start) % padded
    ordered = jnp.take(comps, order, axis=1)
    spread = jnp.pad(ordered, ((2 * reach, 2 * reach), (0, 0)), constant_values=NOWHERE)
    near = []
    offsets = [0]
    for distance in range(1, reach + 1):
        offsets += [-distance, distance]
    for offset in offsets:
        for who in range(2):
            index = (group + offset + reach) * 2 + (member if who == 0 else 1 - member)
            near.append(lax.dynamic_index_in_dim(spread, index, 0, keepdims=False))
    near = jnp.concatenate(near)
    home = near[: 2 * padded]

    padded_spectrum = jnp.pad(spectrum, ((0, padded - slots), (0, 0), (0, 0)))
    sent = lax.dynamic_slice_in_dim(padded_spectrum, rest - own_start, handled, axis=0)
    other = lax.ppermute(sent.astype(jnp.bfloat16), "lon", swap)
    terrain = jnp.stack([water_depth, sea_mask.astype(jnp.float32)])
    terrain = jnp.concatenate([terrain, lax.ppermute(terrain, "lon", swap)], axis=2)
    depth, ocean = terrain[0], terrain[1]
    face_x = 0.5 * ocean * jnp.roll(ocean, -1, axis=1)
    face_y = 0.5 * ocean * jnp.pad(ocean[1:], ((0, 1), (0, 0)))

    held = near[:handled]
    real = held >= 0
    held = jnp.where(real, held, 0)
    held_freq = held // NDIR
    wavenumber = (2.0 * math.pi * frequency_of(held_freq)) ** 2 / 9.81
    heading = heading_of(held % NDIR)
    count = jnp.where(real, jnp.take(substeps, held_freq), 0)
    params = jnp.stack(
        [
            over_lanes(values, half)
            for values in (
                wavenumber,
                jnp.cos(heading),
                jnp.sin(heading),
                count.astype(jnp.float32),
            )
        ]
    )
    most = jnp.max(count.reshape(handled // ROUND, ROUND), axis=1)
    block_place = (own_start // ROUND).astype(jnp.int32)
    mine, foreign = advance(
        block_place[None],
        most,
        padded_spectrum,
        other,
        depth[:, None],
        ocean[:, None],
        face_x[:, None],
        face_y[:, None],
        params,
    )
    returned = lax.ppermute(
        lax.dynamic_slice_in_dim(foreign, lon_place * (handled - rest), rest, axis=1), "lon", swap
    )
    natural = jnp.concatenate([mine, returned], axis=1)

    home_safe = jnp.where(home >= 0, home, 0)
    home_heading = heading_of(home_safe % NDIR)
    home_scale = jnp.sqrt(frequency_of(home_safe // NDIR) / 0.2)
    scales = jnp.stack(
        [
            over_lanes(home_scale * jnp.cos(home_heading), half),
            over_lanes(home_scale * jnp.sin(home_heading), half),
        ]
    )
    directions = jnp.arange(NDIR, dtype=jnp.int32)
    home_dir = (home[:, None] % NDIR == directions[None]).astype(jnp.bfloat16)
    near_dir = (near[:, None] % NDIR == directions[None]).astype(jnp.bfloat16)
    gap = near[None] // NDIR - home[:, None] // NDIR
    matrix = None
    for index in range(5):
        rows = jnp.dot(home_dir, coupling[index], preferred_element_type=jnp.bfloat16)
        term = jnp.dot(rows, near_dir.T, preferred_element_type=jnp.bfloat16)
        term = jnp.where(gap == index - 2, term, jnp.zeros_like(term))
        matrix = term if matrix is None else matrix + term

    part_rows = lat // 2
    chunk_rows = part_rows // CHUNKS
    changes = [[], []]
    for chunk in range(CHUNKS):
        start = member * part_rows + chunk * chunk_rows
        far_start = (1 - member) * part_rows + chunk * chunk_rows
        own = lax.dynamic_slice_in_dim(natural, start, chunk_rows, axis=0)
        far = lax.dynamic_slice_in_dim(natural, far_start, chunk_rows, axis=0)
        paired = lax.ppermute(far, "comp", pairs)
        inputs = [own, paired]
        for distance in range(1, reach + 1):
            step = 2 * distance
            up = [(i, i + step) for i in range(comp_count - step)]
            down = [(i + step, i) for i in range(comp_count - step)]
            for route in (up, down):
                for block in (own, paired):
                    inputs.append(lax.ppermute(block, "comp", route))
        wind = lax.dynamic_slice_in_dim(wind_field, start, chunk_rows, axis=1)[:, :, None]
        kept, sent_back = sources(matrix, scales, wind, inputs)
        changes[0].append(kept)
        changes[1].append(lax.ppermute(sent_back, "comp", pairs))

    out_place = jnp.stack([block_place, member.astype(jnp.int32)])
    return finish(out_place, natural, changes[0] + changes[1])[:slots]


def solution(mesh):
    in_specs = (
        P(("grp", "comp"), None, "lon"),
        P(None, "lon"),
        P(None, "lon"),
        P(None, "grp", "lon"),
        P(),
        P(),
        P(),
    )
    out_specs = P(("grp", "comp"), None, "lon")
    return jax.shard_map(
        on_device, mesh=mesh, in_specs=in_specs, out_specs=out_specs, check_vma=False
    )
```

```python
import functools
import math

import jax
import jax.numpy as jnp
from jax import lax
from jax.experimental import pallas as pl
from jax.experimental.pallas import tpu as pltpu
from jax.sharding import PartitionSpec as P

NDIR = 36
NFREQ = 32
ROUND = 16
UNROLL = 16
UNROLL_C = 4
CHUNKS = 2
REACH = 8
NOWHERE = -100000
VMEM = 48 * 1024 * 1024


def round_up(value, step):
    return (value + step - 1) // step * step


def depth_speed(scaled):
    value = jnp.tanh(scaled)
    return 0.8 * value * lax.rsqrt(value)


def face_weights(c):
    forward = c >= 0.0
    first = 0.5 * c * (1.0 + c)
    third = first * (1.0 - c) * (1.0 / 3.0)
    behind = jnp.where(forward, third, 0.0)
    beyond = third - behind
    return (
        -behind,
        first + 2.0 * behind - beyond,
        c - first + 2.0 * beyond - behind,
        -beyond,
    )


def cell_weights(right, left):
    return (
        left[0],
        left[1] - right[0],
        1.0 - right[1] + left[2],
        left[3] - right[2],
        -right[3],
    )


def advect_kernel(
    place, steps, mine, other, depth, ocean, face_x, face_left, face_y, params, out_mine, out_other,
    q, r, *taps
):
    lat = depth.shape[0]
    width = depth.shape[2]
    half = width // 2
    shape = (1, ROUND, width)
    wave = jnp.broadcast_to(params[0][:, :1][None], shape)
    east = jnp.broadcast_to(params[1][:, :1][None], shape)
    north = jnp.broadcast_to(params[2][:, :1][None], shape)
    count = jnp.broadcast_to(params[3][:, :1][None], shape)
    taps_x, taps_y = taps[:5], taps[5:]
    r[0:2] = jnp.zeros((2, ROUND, width), jnp.float32)
    r[lat + 2 : lat + 4] = jnp.zeros((2, ROUND, width), jnp.float32)
    q[:, :, 0:half] = jnp.swapaxes(mine[...], 0, 1)
    q[:, :, half:width] = jnp.swapaxes(other[...].astype(jnp.float32), 0, 1)

    def prepare(i, carry):
        row = pl.ds(i, 1)
        sea = ocean[row]
        r[pl.ds(i + 2, 1)] = depth_speed(wave * depth[row]) * sea
        q[row] = q[row] * sea
        return carry

    lax.fori_loop(0, lat, prepare, 0, unroll=UNROLL)

    def coefficients(i, below):
        row = pl.ds(i, 1)
        speed = r[pl.ds(i + 2, 1)]
        above = r[pl.ds(i + 3, 1)]
        right = (speed + pltpu.roll(speed, width - 1, 2)) * east * face_x[row]
        left = (speed + pltpu.roll(speed, 1, 2)) * east * face_left[row]
        for tap, value in zip(taps_x, cell_weights(face_weights(right), face_weights(left))):
            tap[row] = value
        weights = face_weights((speed + above) * north * face_y[row])
        for tap, value in zip(taps_y, cell_weights(weights, below)):
            tap[row] = value
        return weights

    none = jnp.zeros(shape, jnp.float32)
    lax.fori_loop(0, lat, coefficients, (none,) * 4, unroll=UNROLL_C)

    def substep(t, carry):
        def along_x(i, inner):
            row = pl.ds(i, 1)
            here = q[row]
            total = taps_x[2][row] * here
            for tap, shift in ((0, 2), (1, 1), (3, width - 1), (4, width - 2)):
                total = total + taps_x[tap][row] * pltpu.roll(here, shift, 2)
            r[pl.ds(i + 2, 1)] = total
            return inner

        lax.fori_loop(0, lat, along_x, 0, unroll=UNROLL)
        active = count > t.astype(jnp.float32)

        def along_y(i, inner):
            row = pl.ds(i, 1)
            total = taps_y[0][row] * r[row]
            for tap in range(1, 5):
                total = total + taps_y[tap][row] * r[pl.ds(i + tap, 1)]
            q[row] = jnp.where(active, total, q[row])
            return inner

        lax.fori_loop(0, lat, along_y, 0, unroll=UNROLL)
        return carry

    lax.fori_loop(0, steps[pl.program_id(0)], substep, 0)
    out_mine[...] = q[:, :, 0:half].astype(jnp.bfloat16)
    out_other[...] = q[:, :, half:width].astype(jnp.bfloat16)


def advance(place, steps, mine, other, depth, ocean, face_x, face_left, face_y, params):
    handled, lat, half = other.shape
    whole = pl.BlockSpec((lat, 1, 2 * half), lambda i, place, steps: (0, 0, 0))
    field = pltpu.VMEM((lat, ROUND, 2 * half), jnp.float32)
    out = pl.BlockSpec((lat, ROUND, half), lambda i, place, steps: (0, i, 0))
    shape = jax.ShapeDtypeStruct((lat, handled, half), jnp.bfloat16)
    return pl.pallas_call(
        advect_kernel,
        grid_spec=pltpu.PrefetchScalarGridSpec(
            num_scalar_prefetch=2,
            grid=(handled // ROUND,),
            in_specs=[
                pl.BlockSpec((ROUND, lat, half), lambda i, place, steps: (i + place[0], 0, 0)),
                pl.BlockSpec((ROUND, lat, half), lambda i, place, steps: (i, 0, 0)),
                whole,
                whole,
                whole,
                whole,
                whole,
                pl.BlockSpec((4, ROUND, half), lambda i, place, steps: (0, i, 0)),
            ],
            out_specs=[out, out],
            scratch_shapes=[
                field,
                pltpu.VMEM((lat + 4, ROUND, 2 * half), jnp.float32),
            ]
            + [field] * 10,
        ),
        out_shape=[shape, shape],
        compiler_params=pltpu.CompilerParams(vmem_limit_bytes=VMEM),
        cost_estimate=pl.CostEstimate(
            flops=120 * handled * lat * half * 2,
            bytes_accessed=10 * handled * lat * half * 2,
            transcendentals=0,
        ),
        name="advance",
    )(place, steps, mine, other, depth, ocean, face_x, face_left, face_y, params)


def source_kernel(pieces, matrix, scales, wind, *refs):
    inputs, outputs = refs[:pieces], refs[pieces:]
    slots = inputs[0].shape[1]

    def pair(ref):
        return jnp.concatenate([ref[0], ref[1]], axis=1)

    def twice(ref):
        return jnp.concatenate([ref, ref], axis=1)

    near = jnp.concatenate([pair(ref) for ref in inputs], axis=0)
    wide = near.astype(jnp.float32)
    square = (wide * wide).astype(jnp.bfloat16)
    wind_east = jnp.concatenate([wind[0, 0], wind[0, 1]], axis=1)
    wind_north = jnp.concatenate([wind[1, 0], wind[1, 1]], axis=1)
    half = inputs[0].shape[2]
    for part in range(2):
        rows = slice(part * slots, part * slots + slots)
        linear_part = jnp.dot(matrix[rows, :], near, preferred_element_type=jnp.float32)
        square_part = jnp.dot(matrix[rows, :], square, preferred_element_type=jnp.float32)
        energy = wide[rows]
        push = twice(scales[0, rows]) * wind_east + twice(scales[1, rows]) * wind_north
        rate = 0.3 * jnp.maximum(0.0, push - 1.0)
        transfer = 0.5 * (energy * square_part - energy * energy * linear_part)
        change = (0.5 * (rate * energy + transfer)).astype(jnp.bfloat16)
        outputs[part][0] = change[:, :half]
        outputs[part][1] = change[:, half:]


def sources(matrix, scales, wind, inputs):
    rows, slots, half = inputs[0].shape
    block = pl.BlockSpec((2, slots, half), lambda i: (i, 0, 0))
    shape = jax.ShapeDtypeStruct((rows, slots, half), jnp.bfloat16)
    return pl.pallas_call(
        functools.partial(source_kernel, len(inputs)),
        grid=(rows // 2,),
        in_specs=[
            pl.BlockSpec(matrix.shape, lambda i: (0, 0)),
            pl.BlockSpec(scales.shape, lambda i: (0, 0, 0)),
            pl.BlockSpec((2, 2, 1, half), lambda i: (0, i, 0, 0)),
        ]
        + [block] * len(inputs),
        out_specs=[block, block],
        out_shape=[shape, shape],
        compiler_params=pltpu.CompilerParams(vmem_limit_bytes=VMEM),
        cost_estimate=pl.CostEstimate(
            flops=4 * matrix.size * rows * half,
            bytes_accessed=2 * (len(inputs) + 2) * rows * slots * half,
            transcendentals=0,
        ),
        name="sources",
    )(matrix, scales, wind, *inputs)


def finish_kernel(chunks, place, natural, *refs):
    changes, out = refs[: 2 * chunks], refs[2 * chunks]
    part_rows = natural.shape[0] // 2
    chunk_rows = part_rows // chunks
    for which in range(2):
        part = place[1] if which == 0 else 1 - place[1]
        start = pl.multiple_of(part * part_rows, 8)
        change = jnp.concatenate(
            [changes[which * chunks + chunk][...] for chunk in range(chunks)], axis=0
        ).astype(jnp.float32)
        total = natural[pl.ds(start, part_rows)].astype(jnp.float32) + change
        out[:, pl.ds(start, part_rows), :] = jnp.swapaxes(total, 0, 1)


def finish(place, natural, changes):
    lat, slots, half = natural.shape
    blocks = slots // ROUND
    return pl.pallas_call(
        functools.partial(finish_kernel, len(changes) // 2),
        grid_spec=pltpu.PrefetchScalarGridSpec(
            num_scalar_prefetch=1,
            grid=(blocks,),
            in_specs=[pl.BlockSpec((lat, ROUND, half), lambda i, place: (0, i, 0))]
            + [
                pl.BlockSpec((change.shape[0], ROUND, half), lambda i, place: (0, i, 0))
                for change in changes
            ],
            out_specs=pl.BlockSpec(
                (ROUND, lat, half), lambda i, place: (lax.rem(i + place[0], blocks), 0, 0)
            ),
        ),
        out_shape=jax.ShapeDtypeStruct((slots, lat, half), jnp.float32),
        compiler_params=pltpu.CompilerParams(vmem_limit_bytes=VMEM),
        name="finish",
    )(place, natural, *changes)


def frequency_of(index):
    return 0.0418 * jnp.power(1.1, index.astype(jnp.float32))


def heading_of(index):
    return 2.0 * math.pi * (index.astype(jnp.float32) + 0.5) / NDIR


def over_lanes(values, lanes):
    return jnp.broadcast_to(values[:, None], (values.shape[0], lanes))


def on_device(spectrum, water_depth, sea_mask, wind_field, slot_comp, substeps, coupling):
    slots, lat, half = spectrum.shape
    comp_count = lax.axis_size("comp")
    groups = comp_count // 2
    padded = round_up(slots, ROUND)
    handled = round_up(padded // 2, ROUND)
    rest = padded - handled
    comp_place = lax.axis_index("comp")
    lon_place = lax.axis_index("lon")
    member = comp_place % 2
    group = comp_place // 2
    places = 2 * NFREQ // comp_count
    reach = (REACH + places - 1) // places
    swap = [(0, 1), (1, 0)]
    pairs = [(i, i ^ 1) for i in range(comp_count)]

    comps = jnp.pad(
        slot_comp.reshape(comp_count, slots),
        ((0, 0), (0, padded - slots)),
        constant_values=NOWHERE,
    )
    own_start = lon_place * rest
    order = (jnp.arange(padded, dtype=jnp.int32) + own_start) % padded
    ordered = jnp.take(comps, order, axis=1)
    spread = jnp.pad(ordered, ((2 * reach, 2 * reach), (0, 0)), constant_values=NOWHERE)
    near = []
    offsets = [0]
    for distance in range(1, reach + 1):
        offsets += [-distance, distance]
    for offset in offsets:
        for who in range(2):
            index = (group + offset + reach) * 2 + (member if who == 0 else 1 - member)
            near.append(lax.dynamic_index_in_dim(spread, index, 0, keepdims=False))
    near = jnp.concatenate(near)
    home = near[: 2 * padded]

    padded_spectrum = jnp.pad(spectrum, ((0, padded - slots), (0, 0), (0, 0)))
    sent = lax.dynamic_slice_in_dim(padded_spectrum, rest - own_start, handled, axis=0)
    other = lax.ppermute(sent.astype(jnp.bfloat16), "lon", swap)
    terrain = jnp.stack([water_depth, sea_mask.astype(jnp.float32)])
    terrain = jnp.concatenate([terrain, lax.ppermute(terrain, "lon", swap)], axis=2)
    depth, ocean = terrain[0], terrain[1]
    face_x = 0.5 * ocean * jnp.roll(ocean, -1, axis=1)
    face_y = 0.5 * ocean * jnp.pad(ocean[1:], ((0, 1), (0, 0)))

    held = near[:handled]
    real = held >= 0
    held = jnp.where(real, held, 0)
    held_freq = held // NDIR
    wavenumber = (2.0 * math.pi * frequency_of(held_freq)) ** 2 / 9.81
    heading = heading_of(held % NDIR)
    count = jnp.where(real, jnp.take(substeps, held_freq), 0)
    params = jnp.stack(
        [
            over_lanes(values, half)
            for values in (
                wavenumber,
                jnp.cos(heading),
                jnp.sin(heading),
                count.astype(jnp.float32),
            )
        ]
    )
    most = jnp.max(count.reshape(handled // ROUND, ROUND), axis=1)
    block_place = (own_start // ROUND).astype(jnp.int32)
    mine, foreign = advance(
        block_place[None],
        most,
        padded_spectrum,
        other,
        depth[:, None],
        ocean[:, None],
        face_x[:, None],
        jnp.roll(face_x, 1, axis=1)[:, None],
        face_y[:, None],
        params,
    )
    returned = lax.ppermute(
        lax.dynamic_slice_in_dim(foreign, lon_place * (handled - rest), rest, axis=1), "lon", swap
    )
    natural = jnp.concatenate([mine, returned], axis=1)

    home_safe = jnp.where(home >= 0, home, 0)
    home_heading = heading_of(home_safe % NDIR)
    home_scale = jnp.sqrt(frequency_of(home_safe // NDIR) / 0.2)
    scales = jnp.stack(
        [
            over_lanes(home_scale * jnp.cos(home_heading), half),
            over_lanes(home_scale * jnp.sin(home_heading), half),
        ]
    )
    directions = jnp.arange(NDIR, dtype=jnp.int32)
    home_dir = (home[:, None] % NDIR == directions[None]).astype(jnp.bfloat16)
    near_dir = (near[:, None] % NDIR == directions[None]).astype(jnp.bfloat16)
    gap = near[None] // NDIR - home[:, None] // NDIR
    matrix = None
    for index in range(5):
        rows = jnp.dot(home_dir, coupling[index], preferred_element_type=jnp.bfloat16)
        term = jnp.dot(rows, near_dir.T, preferred_element_type=jnp.bfloat16)
        term = jnp.where(gap == index - 2, term, jnp.zeros_like(term))
        matrix = term if matrix is None else matrix + term

    part_rows = lat // 2
    chunk_rows = part_rows // CHUNKS
    changes = [[], []]
    for chunk in range(CHUNKS):
        start = member * part_rows + chunk * chunk_rows
        far_start = (1 - member) * part_rows + chunk * chunk_rows
        own = lax.dynamic_slice_in_dim(natural, start, chunk_rows, axis=0)
        far = lax.dynamic_slice_in_dim(natural, far_start, chunk_rows, axis=0)
        paired = lax.ppermute(far, "comp", pairs)
        inputs = [own, paired]
        for distance in range(1, reach + 1):
            step = 2 * distance
            up = [(i, i + step) for i in range(comp_count - step)]
            down = [(i + step, i) for i in range(comp_count - step)]
            for route in (up, down):
                for block in (own, paired):
                    inputs.append(lax.ppermute(block, "comp", route))
        wind = lax.dynamic_slice_in_dim(wind_field, start, chunk_rows, axis=1)[:, :, None]
        kept, sent_back = sources(matrix, scales, wind, inputs)
        changes[0].append(kept)
        changes[1].append(lax.ppermute(sent_back, "comp", pairs))

    out_place = jnp.stack([block_place, member.astype(jnp.int32)])
    return finish(out_place, natural, changes[0] + changes[1])[:slots]


def solution(mesh):
    in_specs = (
        P(("grp", "comp"), None, "lon"),
        P(None, "lon"),
        P(None, "lon"),
        P(None, "grp", "lon"),
        P(),
        P(),
        P(),
    )
    out_specs = P(("grp", "comp"), None, "lon")
    return jax.shard_map(
        on_device, mesh=mesh, in_specs=in_specs, out_specs=out_specs, check_vma=False
    )
```

```python
import functools
import math

import jax
import jax.numpy as jnp
from jax import lax
from jax.experimental import pallas as pl
from jax.experimental.pallas import tpu as pltpu
from jax.sharding import PartitionSpec as P

NDIR = 36
NFREQ = 32
ROUND = 16
UNROLL = 16
UNROLL_C = 4
CHUNKS = 3
REACH = 8
NOWHERE = -100000
VMEM = 48 * 1024 * 1024


def round_up(value, step):
    return (value + step - 1) // step * step


def depth_speed(scaled):
    value = jnp.tanh(scaled)
    return 0.8 * value * lax.rsqrt(value)


def face_weights(c):
    forward = c >= 0.0
    first = 0.5 * c * (1.0 + c)
    third = first * (1.0 - c) * (1.0 / 3.0)
    behind = jnp.where(forward, third, 0.0)
    beyond = third - behind
    return (
        -behind,
        first + 2.0 * behind - beyond,
        c - first + 2.0 * beyond - behind,
        -beyond,
    )


def cell_weights(right, left):
    return (
        left[0],
        left[1] - right[0],
        1.0 - right[1] + left[2],
        left[3] - right[2],
        -right[3],
    )


def advect_kernel(
    table, steps, mine, other, depth, ocean, face_x, face_left, face_y, params,
    keep, over_lon, over_pair, over_both, q, r, *taps
):
    lat = depth.shape[0]
    width = depth.shape[2]
    half = width // 2
    shape = (1, ROUND, width)
    wave = jnp.broadcast_to(params[0][:, :1][None], shape)
    east = jnp.broadcast_to(params[1][:, :1][None], shape)
    north = jnp.broadcast_to(params[2][:, :1][None], shape)
    count = jnp.broadcast_to(params[3][:, :1][None], shape)
    taps_x, taps_y = taps[:5], taps[5:]
    r[0:2] = jnp.zeros((2, ROUND, width), jnp.float32)
    r[lat + 2 : lat + 4] = jnp.zeros((2, ROUND, width), jnp.float32)
    q[:, :, 0:half] = jnp.swapaxes(mine[...], 0, 1)
    q[:, :, half:width] = jnp.swapaxes(other[...].astype(jnp.float32), 0, 1)

    def prepare(i, carry):
        row = pl.ds(i, 1)
        sea = ocean[row]
        r[pl.ds(i + 2, 1)] = depth_speed(wave * depth[row]) * sea
        q[row] = q[row] * sea
        return carry

    lax.fori_loop(0, lat, prepare, 0, unroll=UNROLL)

    def coefficients(i, below):
        row = pl.ds(i, 1)
        speed = r[pl.ds(i + 2, 1)]
        above = r[pl.ds(i + 3, 1)]
        right = (speed + pltpu.roll(speed, width - 1, 2)) * east * face_x[row]
        left = (speed + pltpu.roll(speed, 1, 2)) * east * face_left[row]
        for tap, value in zip(taps_x, cell_weights(face_weights(right), face_weights(left))):
            tap[row] = value
        weights = face_weights((speed + above) * north * face_y[row])
        for tap, value in zip(taps_y, cell_weights(weights, below)):
            tap[row] = value
        return weights

    none = jnp.zeros(shape, jnp.float32)
    lax.fori_loop(0, lat, coefficients, (none,) * 4, unroll=UNROLL_C)

    def substep(t, carry):
        def along_x(i, inner):
            row = pl.ds(i, 1)
            here = q[row]
            total = taps_x[2][row] * here
            for tap, shift in ((0, 2), (1, 1), (3, width - 1), (4, width - 2)):
                total = total + taps_x[tap][row] * pltpu.roll(here, shift, 2)
            r[pl.ds(i + 2, 1)] = total
            return inner

        lax.fori_loop(0, lat, along_x, 0, unroll=UNROLL)
        active = count > t.astype(jnp.float32)

        def along_y(i, inner):
            row = pl.ds(i, 1)
            total = taps_y[0][row] * r[row]
            for tap in range(1, 5):
                total = total + taps_y[tap][row] * r[pl.ds(i + tap, 1)]
            q[row] = jnp.where(active, total, q[row])
            return inner

        lax.fori_loop(0, lat, along_y, 0, unroll=UNROLL)
        return carry

    lax.fori_loop(0, steps[0], substep, 0)
    part_rows = lat // 2
    here = pl.ds(table[1] * part_rows, part_rows)
    there = pl.ds((1 - table[1]) * part_rows, part_rows)
    keep[...] = q[here, :, 0:half].astype(jnp.bfloat16)
    over_lon[...] = q[here, :, half:width].astype(jnp.bfloat16)
    over_pair[...] = q[there, :, 0:half].astype(jnp.bfloat16)
    over_both[...] = q[there, :, half:width].astype(jnp.bfloat16)


def advance(table, steps, mine, other, block, fields, params):
    _, lat, half = other.shape
    whole = pl.BlockSpec((lat, 1, 2 * half), lambda i, table, steps: (0, 0, 0))
    field = pltpu.VMEM((lat, ROUND, 2 * half), jnp.float32)
    out = pl.BlockSpec((lat // 2, ROUND, half), lambda i, table, steps: (0, 0, 0))
    shape = jax.ShapeDtypeStruct((lat // 2, ROUND, half), jnp.bfloat16)
    return pl.pallas_call(
        advect_kernel,
        grid_spec=pltpu.PrefetchScalarGridSpec(
            num_scalar_prefetch=2,
            grid=(1,),
            in_specs=[
                pl.BlockSpec((ROUND, lat, half), lambda i, table, steps: (table[0], 0, 0)),
                pl.BlockSpec((ROUND, lat, half), lambda i, table, steps: (block, 0, 0)),
            ]
            + [whole] * len(fields)
            + [pl.BlockSpec(params.shape, lambda i, table, steps: (0, 0, 0))],
            out_specs=[out] * 4,
            scratch_shapes=[
                field,
                pltpu.VMEM((lat + 4, ROUND, 2 * half), jnp.float32),
            ]
            + [field] * 10,
        ),
        out_shape=[shape] * 4,
        compiler_params=pltpu.CompilerParams(vmem_limit_bytes=VMEM),
        cost_estimate=pl.CostEstimate(
            flops=60000 * ROUND * lat * half // 8,
            bytes_accessed=10 * ROUND * lat * half,
            transcendentals=0,
        ),
        name="advance",
    )(table, steps, mine, other, *fields, params)


def source_kernel(spans, matrix, scales, wind, *refs):
    inputs, outputs = refs[: len(spans)], refs[len(spans) :]
    half = inputs[0].shape[2]
    slots = outputs[0].shape[1]

    def pair(ref):
        return jnp.concatenate([ref[0], ref[1]], axis=1)

    def twice(value):
        return jnp.concatenate([value, value], axis=1)

    near = jnp.concatenate([pair(ref) for ref in inputs], axis=0)
    wide = near.astype(jnp.float32)
    square = (wide * wide).astype(jnp.bfloat16)
    wind_east = jnp.concatenate([wind[0, 0], wind[0, 1]], axis=1)
    wind_north = jnp.concatenate([wind[1, 0], wind[1, 1]], axis=1)
    for part in (1, 0):
        rows = slice(part * slots, part * slots + slots)
        linear_part = jnp.dot(matrix[rows, :], near, preferred_element_type=jnp.float32)
        square_part = jnp.dot(matrix[rows, :], square, preferred_element_type=jnp.float32)
        energy = []
        start = 0
        for size, is_home in spans:
            if is_home:
                first = start + part * (size // 2)
                energy.append(wide[first : first + size // 2])
            start += size
        energy = jnp.concatenate(energy, axis=0)
        push = twice(scales[0, rows]) * wind_east + twice(scales[1, rows]) * wind_north
        rate = 0.3 * jnp.maximum(0.0, push - 1.0)
        transfer = 0.5 * (energy * square_part - energy * energy * linear_part)
        change = (0.5 * (rate * energy + transfer)).astype(jnp.bfloat16)
        total = (energy + change.astype(jnp.float32)).astype(jnp.bfloat16)
        outputs[part][0] = total[:, :half]
        outputs[part][1] = total[:, half:]


def sources(matrix, scales, wind, inputs, homes, first, rows):
    half = inputs[0].shape[2]
    slots = matrix.shape[0] // 2
    base = first // 2
    spans = tuple((block.shape[1], home) for block, home in zip(inputs, homes))
    out = pl.BlockSpec((2, slots, half), lambda i: (i, 0, 0))
    shape = jax.ShapeDtypeStruct((rows, slots, half), jnp.bfloat16)
    return pl.pallas_call(
        functools.partial(source_kernel, spans),
        grid=(rows // 2,),
        in_specs=[
            pl.BlockSpec(matrix.shape, lambda i: (0, 0)),
            pl.BlockSpec(scales.shape, lambda i: (0, 0, 0)),
            pl.BlockSpec((2, 2, 1, half), lambda i: (0, i + base, 0, 0)),
        ]
        + [pl.BlockSpec((2, size, half), lambda i: (i + base, 0, 0)) for size, _ in spans],
        out_specs=[out, out],
        out_shape=[shape, shape],
        compiler_params=pltpu.CompilerParams(vmem_limit_bytes=VMEM),
        cost_estimate=pl.CostEstimate(
            flops=16 * matrix.size * rows * half,
            bytes_accessed=2 * (matrix.shape[1] + 2 * slots) * rows * half,
            transcendentals=0,
        ),
        name="sources",
    )(matrix, scales, wind, *inputs)


def finish_kernel(chunks, table, *refs):
    values, out = refs[: 2 * chunks], refs[2 * chunks]
    part_rows = out.shape[1] // 2
    member = table[table.shape[0] - 1]
    for which in range(2):
        part = member if which == 0 else 1 - member
        start = pl.multiple_of(part * part_rows, 8)
        total = jnp.concatenate(
            [values[which * chunks + chunk][...] for chunk in range(chunks)], axis=0
        ).astype(jnp.float32)
        out[:, pl.ds(start, part_rows), :] = jnp.swapaxes(total, 0, 1)


def finish(table, values, lat):
    _, slots, half = values[0].shape
    return pl.pallas_call(
        functools.partial(finish_kernel, len(values) // 2),
        grid_spec=pltpu.PrefetchScalarGridSpec(
            num_scalar_prefetch=1,
            grid=(slots // ROUND,),
            in_specs=[
                pl.BlockSpec((value.shape[0], ROUND, half), lambda i, table: (0, i, 0))
                for value in values
            ],
            out_specs=pl.BlockSpec((ROUND, lat, half), lambda i, table: (table[i], 0, 0)),
        ),
        out_shape=jax.ShapeDtypeStruct((slots, lat, half), jnp.float32),
        compiler_params=pltpu.CompilerParams(vmem_limit_bytes=VMEM),
        name="finish",
    )(table, *values)


def frequency_of(index):
    return 0.0418 * jnp.power(1.1, index.astype(jnp.float32))


def heading_of(index):
    return 2.0 * math.pi * (index.astype(jnp.float32) + 0.5) / NDIR


def over_lanes(values, lanes):
    return jnp.broadcast_to(values[:, None], (values.shape[0], lanes))


def on_device(spectrum, water_depth, sea_mask, wind_field, slot_comp, substeps, coupling):
    slots, lat, half = spectrum.shape
    comp_count = lax.axis_size("comp")
    groups = comp_count // 2
    padded = round_up(slots, ROUND)
    handled = round_up(padded // 2, ROUND)
    rest = padded - handled
    comp_place = lax.axis_index("comp")
    lon_place = lax.axis_index("lon")
    member = comp_place % 2
    group = comp_place // 2
    places = 2 * NFREQ // comp_count
    reach = (REACH + places - 1) // places
    swap = [(0, 1), (1, 0)]
    pairs = [(i, i ^ 1) for i in range(comp_count)]

    blocks, handled_blocks, rest_blocks = padded // ROUND, handled // ROUND, rest // ROUND
    comps = jnp.pad(
        slot_comp.reshape(comp_count, slots),
        ((0, 0), (0, padded - slots)),
        constant_values=NOWHERE,
    ).reshape(comp_count, blocks, ROUND)
    spread = jnp.pad(comps, ((2 * reach, 2 * reach), (0, 0), (0, 0)), constant_values=NOWHERE)
    block_of = [[], []]
    for turn in range(handled_blocks):
        block_of[0].append(turn)
        block_of[1].append(turn + handled_blocks if turn < rest_blocks else turn)
    held_blocks = jnp.where(lon_place == 0, jnp.array(block_of[0]), jnp.array(block_of[1]))
    order = []
    for turn in range(handled_blocks):
        order.append((block_of[0][turn], block_of[1][turn]))
        if turn < rest_blocks:
            order.append((block_of[1][turn], block_of[0][turn]))
    pairs_of = jnp.array(order)
    held_order = jnp.where(lon_place == 0, pairs_of[:, 0], pairs_of[:, 1])
    sizes = [2 if turn < rest_blocks else 1 for turn in range(handled_blocks)]
    offsets = [0]
    for distance in range(1, reach + 1):
        offsets += [-distance, distance]

    def held_by(offset, who):
        index = (group + offset + reach) * 2 + (member if who == 0 else 1 - member)
        return jnp.take(lax.dynamic_index_in_dim(spread, index, 0, keepdims=False), held_order, axis=0)

    held_of = {(offset, who): held_by(offset, who) for offset in offsets for who in range(2)}
    near = []
    start = 0
    for size in sizes:
        for offset in offsets:
            for who in range(2):
                near.append(held_of[offset, who][start : start + size].reshape(-1))
        start += size
    near = jnp.concatenate(near)
    home = jnp.concatenate([held_of[0, who].reshape(-1) for who in range(2)])

    padded_spectrum = jnp.pad(spectrum, ((0, padded - slots), (0, 0), (0, 0)))

    def to_send(low, high):
        zero_takes = padded_spectrum[block_of[0][low] * ROUND :][: (high - low) * ROUND]
        one_takes = jnp.concatenate(
            [
                padded_spectrum[block * ROUND : (block + 1) * ROUND]
                for block in block_of[1][low:high]
            ]
        )
        chosen = jnp.where(lon_place == 0, one_takes, zero_takes)
        return lax.ppermute(chosen.astype(jnp.bfloat16), "lon", swap)

    terrain = jnp.stack([water_depth, sea_mask.astype(jnp.float32)])
    terrain = jnp.concatenate([terrain, lax.ppermute(terrain, "lon", swap)], axis=2)
    first_other = to_send(0, 1)
    rest_other = to_send(1, handled_blocks) if handled_blocks > 1 else None
    depth, ocean = terrain[0], terrain[1]
    face_x = 0.5 * ocean * jnp.roll(ocean, -1, axis=1)
    face_left = jnp.roll(face_x, 1, axis=1)
    face_y = 0.5 * ocean * jnp.pad(ocean[1:], ((0, 1), (0, 0)))
    fields = [value[:, None] for value in (depth, ocean, face_x, face_left, face_y)]

    own_comps = lax.dynamic_index_in_dim(comps, comp_place, 0, keepdims=False)
    held = jnp.take(own_comps, held_blocks, axis=0)
    real = held >= 0
    held = jnp.where(real, held, 0)
    held_freq = held // NDIR
    wavenumber = (2.0 * math.pi * frequency_of(held_freq)) ** 2 / 9.81
    heading = heading_of(held % NDIR)
    count = jnp.where(real, jnp.take(substeps, held_freq), 0)
    params = jnp.stack(
        [wavenumber, jnp.cos(heading), jnp.sin(heading), count.astype(jnp.float32)], axis=1
    )
    params = jnp.broadcast_to(params[..., None], params.shape + (half,))
    most = jnp.max(count, axis=1)
    both = [(i, j, i ^ 1, 1 - j) for i in range(comp_count) for j in range(2)]
    both = [(i * 2 + j, k * 2 + l) for i, j, k, l in both]

    part_rows = lat // 2
    inputs, homes = [], []
    for turn in range(handled_blocks):
        table = jnp.stack([held_blocks[turn], member]).astype(jnp.int32)
        keep, over_lon, over_pair, over_both = advance(
            table,
            most[turn : turn + 1],
            padded_spectrum,
            first_other if turn == 0 else rest_other,
            max(turn - 1, 0),
            fields,
            params[turn],
        )
        if turn < rest_blocks:
            parts = [
                keep,
                lax.ppermute(over_lon, "lon", swap),
                lax.ppermute(over_pair, "comp", pairs),
                lax.ppermute(over_both, ("comp", "lon"), both),
            ]
        else:
            parts = [keep, lax.ppermute(over_pair, "comp", pairs)]
        block = jnp.concatenate(parts, axis=1)
        inputs.append(block)
        homes.append(True)
        for distance in range(1, reach + 1):
            step = 2 * distance
            up = [(i, i + step) for i in range(comp_count - step)]
            down = [(i + step, i) for i in range(comp_count - step)]
            for route in (up, down):
                inputs.append(lax.ppermute(block, "comp", route))
                homes.append(False)

    home_safe = jnp.where(home >= 0, home, 0)
    home_heading = heading_of(home_safe % NDIR)
    home_scale = jnp.sqrt(frequency_of(home_safe // NDIR) / 0.2)
    scales = jnp.stack(
        [
            over_lanes(home_scale * jnp.cos(home_heading), half),
            over_lanes(home_scale * jnp.sin(home_heading), half),
        ]
    )
    directions = jnp.arange(NDIR, dtype=jnp.int32)
    home_dir = (home[:, None] % NDIR == directions[None]).astype(jnp.bfloat16)
    near_dir = (near[:, None] % NDIR == directions[None]).astype(jnp.bfloat16)
    gap = near[None] // NDIR - home[:, None] // NDIR
    matrix = None
    for index in range(5):
        rows = jnp.dot(home_dir, coupling[index], preferred_element_type=jnp.bfloat16)
        term = jnp.dot(rows, near_dir.T, preferred_element_type=jnp.bfloat16)
        term = jnp.where(gap == index - 2, term, jnp.zeros_like(term))
        matrix = term if matrix is None else matrix + term

    wind = lax.dynamic_slice_in_dim(wind_field, member * part_rows, part_rows, axis=1)[:, :, None]
    chunk_rows = part_rows // CHUNKS
    values = [[], []]
    for chunk in range(CHUNKS):
        kept, sent_back = sources(
            matrix, scales, wind, inputs, homes, chunk * chunk_rows, chunk_rows
        )
        values[0].append(kept)
        values[1].append(lax.ppermute(sent_back, "comp", pairs))
    out_table = jnp.concatenate([held_order, member[None]]).astype(jnp.int32)
    return finish(out_table, values[0] + values[1], lat)[:slots]


def solution(mesh):
    in_specs = (
        P(("grp", "comp"), None, "lon"),
        P(None, "lon"),
        P(None, "lon"),
        P(None, "grp", "lon"),
        P(),
        P(),
        P(),
    )
    out_specs = P(("grp", "comp"), None, "lon")
    return jax.shard_map(
        on_device, mesh=mesh, in_specs=in_specs, out_specs=out_specs, check_vma=False
    )
```

```python
import functools
import math

import jax
import jax.numpy as jnp
from jax import lax
from jax.experimental import pallas as pl
from jax.experimental.pallas import tpu as pltpu
from jax.sharding import PartitionSpec as P

NDIR = 36
NFREQ = 32
ROUND = 16
UNROLL = 16
UNROLL_C = 4
WORK = 400
CHUNKS = 3
REACH = 8
NOWHERE = -100000
VMEM = 48 * 1024 * 1024


def round_up(value, step):
    return (value + step - 1) // step * step


def depth_speed(scaled):
    value = jnp.tanh(scaled)
    return 0.8 * value * lax.rsqrt(value)


def face_weights(c):
    forward = c >= 0.0
    first = 0.5 * c * (1.0 + c)
    third = first * (1.0 - c) * (1.0 / 3.0)
    behind = jnp.where(forward, third, 0.0)
    beyond = third - behind
    return (
        -behind,
        first + 2.0 * behind - beyond,
        c - first + 2.0 * beyond - behind,
        -beyond,
    )


def cell_weights(right, left):
    return (
        left[0],
        left[1] - right[0],
        1.0 - right[1] + left[2],
        left[3] - right[2],
        -right[3],
    )


def advect_kernel(
    table, steps, mine, other, depth, ocean, face_x, face_left, face_y, params,
    keep, over_lon, over_pair, over_both, q, r, *taps
):
    lat = depth.shape[0]
    width = depth.shape[2]
    half = width // 2
    shape = (1, ROUND, width)
    wave = jnp.broadcast_to(params[0][:, :1][None], shape)
    east = jnp.broadcast_to(params[1][:, :1][None], shape)
    north = jnp.broadcast_to(params[2][:, :1][None], shape)
    count = jnp.broadcast_to(params[3][:, :1][None], shape)
    taps_x, taps_y = taps[:5], taps[5:]
    r[0:2] = jnp.zeros((2, ROUND, width), jnp.float32)
    r[lat + 2 : lat + 4] = jnp.zeros((2, ROUND, width), jnp.float32)
    q[:, :, 0:half] = jnp.swapaxes(mine[...], 0, 1)
    q[:, :, half:width] = jnp.swapaxes(other[...].astype(jnp.float32), 0, 1)

    def prepare(i, carry):
        row = pl.ds(i, 1)
        sea = ocean[row]
        r[pl.ds(i + 2, 1)] = depth_speed(wave * depth[row]) * sea
        q[row] = q[row] * sea
        return carry

    lax.fori_loop(0, lat, prepare, 0, unroll=UNROLL)

    def coefficients(i, below):
        row = pl.ds(i, 1)
        speed = r[pl.ds(i + 2, 1)]
        above = r[pl.ds(i + 3, 1)]
        right = (speed + pltpu.roll(speed, width - 1, 2)) * east * face_x[row]
        left = (speed + pltpu.roll(speed, 1, 2)) * east * face_left[row]
        for tap, value in zip(taps_x, cell_weights(face_weights(right), face_weights(left))):
            tap[row] = value
        weights = face_weights((speed + above) * north * face_y[row])
        for tap, value in zip(taps_y, cell_weights(weights, below)):
            tap[row] = value
        return weights

    none = jnp.zeros(shape, jnp.float32)
    lax.fori_loop(0, lat, coefficients, (none,) * 4, unroll=UNROLL_C)

    def substep(t, carry):
        def along_x(i, inner):
            row = pl.ds(i, 1)
            here = q[row]
            total = taps_x[2][row] * here
            for tap, shift in ((0, 2), (1, 1), (3, width - 1), (4, width - 2)):
                total = total + taps_x[tap][row] * pltpu.roll(here, shift, 2)
            r[pl.ds(i + 2, 1)] = total
            return inner

        lax.fori_loop(0, lat, along_x, 0, unroll=UNROLL)
        active = count > t.astype(jnp.float32)

        def along_y(i, inner):
            row = pl.ds(i, 1)
            total = taps_y[0][row] * r[row]
            for tap in range(1, 5):
                total = total + taps_y[tap][row] * r[pl.ds(i + tap, 1)]
            q[row] = jnp.where(active, total, q[row])
            return inner

        lax.fori_loop(0, lat, along_y, 0, unroll=UNROLL)
        return carry

    lax.fori_loop(0, steps[0], substep, 0)
    part_rows = lat // 2
    here = pl.ds(table[1] * part_rows, part_rows)
    there = pl.ds((1 - table[1]) * part_rows, part_rows)
    keep[...] = q[here, :, 0:half].astype(jnp.bfloat16)
    over_lon[...] = q[here, :, half:width].astype(jnp.bfloat16)
    over_pair[...] = q[there, :, 0:half].astype(jnp.bfloat16)
    over_both[...] = q[there, :, half:width].astype(jnp.bfloat16)


def advance(table, steps, mine, other, block, fields, params):
    _, lat, half = other.shape
    whole = pl.BlockSpec((lat, 1, 2 * half), lambda i, table, steps: (0, 0, 0))
    field = pltpu.VMEM((lat, ROUND, 2 * half), jnp.float32)
    out = pl.BlockSpec((lat // 2, ROUND, half), lambda i, table, steps: (0, 0, 0))
    shape = jax.ShapeDtypeStruct((lat // 2, ROUND, half), jnp.bfloat16)
    return pl.pallas_call(
        advect_kernel,
        grid_spec=pltpu.PrefetchScalarGridSpec(
            num_scalar_prefetch=2,
            grid=(1,),
            in_specs=[
                pl.BlockSpec((ROUND, lat, half), lambda i, table, steps: (table[0], 0, 0)),
                pl.BlockSpec((ROUND, lat, half), lambda i, table, steps: (block, 0, 0)),
            ]
            + [whole] * len(fields)
            + [pl.BlockSpec(params.shape, lambda i, table, steps: (0, 0, 0))],
            out_specs=[out] * 4,
            scratch_shapes=[
                field,
                pltpu.VMEM((lat + 4, ROUND, 2 * half), jnp.float32),
            ]
            + [field] * 10,
        ),
        out_shape=[shape] * 4,
        compiler_params=pltpu.CompilerParams(vmem_limit_bytes=VMEM),
        cost_estimate=pl.CostEstimate(
            flops=100 * ROUND * lat * half,
            bytes_accessed=WORK * ROUND * lat * half,
            transcendentals=0,
        ),
        name="advance",
    )(table, steps, mine, other, *fields, params)


def source_kernel(spans, matrix, scales, wind, *refs):
    inputs, outputs = refs[: len(spans)], refs[len(spans) :]
    half = inputs[0].shape[2]
    slots = outputs[0].shape[1]

    def pair(ref):
        return jnp.concatenate([ref[0], ref[1]], axis=1)

    def twice(value):
        return jnp.concatenate([value, value], axis=1)

    near = jnp.concatenate([pair(ref) for ref in inputs], axis=0)
    wide = near.astype(jnp.float32)
    square = (wide * wide).astype(jnp.bfloat16)
    wind_east = jnp.concatenate([wind[0, 0], wind[0, 1]], axis=1)
    wind_north = jnp.concatenate([wind[1, 0], wind[1, 1]], axis=1)
    for part in (1, 0):
        rows = slice(part * slots, part * slots + slots)
        linear_part = jnp.dot(matrix[rows, :], near, preferred_element_type=jnp.float32)
        square_part = jnp.dot(matrix[rows, :], square, preferred_element_type=jnp.float32)
        energy = []
        start = 0
        for size, is_home in spans:
            if is_home:
                first = start + part * (size // 2)
                energy.append(wide[first : first + size // 2])
            start += size
        energy = jnp.concatenate(energy, axis=0)
        push = twice(scales[0, rows]) * wind_east + twice(scales[1, rows]) * wind_north
        rate = 0.3 * jnp.maximum(0.0, push - 1.0)
        transfer = 0.5 * (energy * square_part - energy * energy * linear_part)
        change = (0.5 * (rate * energy + transfer)).astype(jnp.bfloat16)
        total = (energy + change.astype(jnp.float32)).astype(jnp.bfloat16)
        outputs[part][0] = total[:, :half]
        outputs[part][1] = total[:, half:]


def sources(matrix, scales, wind, inputs, homes, first, rows):
    half = inputs[0].shape[2]
    slots = matrix.shape[0] // 2
    base = first // 2
    spans = tuple((block.shape[1], home) for block, home in zip(inputs, homes))
    out = pl.BlockSpec((2, slots, half), lambda i: (i, 0, 0))
    shape = jax.ShapeDtypeStruct((rows, slots, half), jnp.bfloat16)
    return pl.pallas_call(
        functools.partial(source_kernel, spans),
        grid=(rows // 2,),
        in_specs=[
            pl.BlockSpec(matrix.shape, lambda i: (0, 0)),
            pl.BlockSpec(scales.shape, lambda i: (0, 0, 0)),
            pl.BlockSpec((2, 2, 1, half), lambda i: (0, i + base, 0, 0)),
        ]
        + [pl.BlockSpec((2, size, half), lambda i: (i + base, 0, 0)) for size, _ in spans],
        out_specs=[out, out],
        out_shape=[shape, shape],
        compiler_params=pltpu.CompilerParams(vmem_limit_bytes=VMEM),
        cost_estimate=pl.CostEstimate(
            flops=16 * matrix.size * rows * half,
            bytes_accessed=2 * (matrix.shape[1] + 2 * slots) * rows * half,
            transcendentals=0,
        ),
        name="sources",
    )(matrix, scales, wind, *inputs)


def finish_kernel(chunks, table, *refs):
    values, out = refs[: 2 * chunks], refs[2 * chunks]
    part_rows = out.shape[1] // 2
    member = table[table.shape[0] - 1]
    for which in range(2):
        part = member if which == 0 else 1 - member
        start = pl.multiple_of(part * part_rows, 8)
        total = jnp.concatenate(
            [values[which * chunks + chunk][...] for chunk in range(chunks)], axis=0
        ).astype(jnp.float32)
        out[:, pl.ds(start, part_rows), :] = jnp.swapaxes(total, 0, 1)


def finish(table, values, lat):
    _, slots, half = values[0].shape
    return pl.pallas_call(
        functools.partial(finish_kernel, len(values) // 2),
        grid_spec=pltpu.PrefetchScalarGridSpec(
            num_scalar_prefetch=1,
            grid=(slots // ROUND,),
            in_specs=[
                pl.BlockSpec((value.shape[0], ROUND, half), lambda i, table: (0, i, 0))
                for value in values
            ],
            out_specs=pl.BlockSpec((ROUND, lat, half), lambda i, table: (table[i], 0, 0)),
        ),
        out_shape=jax.ShapeDtypeStruct((slots, lat, half), jnp.float32),
        compiler_params=pltpu.CompilerParams(vmem_limit_bytes=VMEM),
        name="finish",
    )(table, *values)


def frequency_of(index):
    return 0.0418 * jnp.power(1.1, index.astype(jnp.float32))


def heading_of(index):
    return 2.0 * math.pi * (index.astype(jnp.float32) + 0.5) / NDIR


def over_lanes(values, lanes):
    return jnp.broadcast_to(values[:, None], (values.shape[0], lanes))


def on_device(spectrum, water_depth, sea_mask, wind_field, slot_comp, substeps, coupling):
    slots, lat, half = spectrum.shape
    comp_count = lax.axis_size("comp")
    groups = comp_count // 2
    padded = round_up(slots, ROUND)
    handled = round_up(padded // 2, ROUND)
    rest = padded - handled
    comp_place = lax.axis_index("comp")
    lon_place = lax.axis_index("lon")
    member = comp_place % 2
    group = comp_place // 2
    places = 2 * NFREQ // comp_count
    reach = (REACH + places - 1) // places
    swap = [(0, 1), (1, 0)]
    pairs = [(i, i ^ 1) for i in range(comp_count)]

    blocks, handled_blocks, rest_blocks = padded // ROUND, handled // ROUND, rest // ROUND
    comps = jnp.pad(
        slot_comp.reshape(comp_count, slots),
        ((0, 0), (0, padded - slots)),
        constant_values=NOWHERE,
    ).reshape(comp_count, blocks, ROUND)
    spread = jnp.pad(comps, ((2 * reach, 2 * reach), (0, 0), (0, 0)), constant_values=NOWHERE)
    block_of = [[], []]
    for turn in range(handled_blocks):
        block_of[0].append(turn)
        block_of[1].append(turn + handled_blocks if turn < rest_blocks else turn)
    held_blocks = jnp.where(lon_place == 0, jnp.array(block_of[0]), jnp.array(block_of[1]))
    order = []
    for turn in range(handled_blocks):
        order.append((block_of[0][turn], block_of[1][turn]))
        if turn < rest_blocks:
            order.append((block_of[1][turn], block_of[0][turn]))
    pairs_of = jnp.array(order)
    held_order = jnp.where(lon_place == 0, pairs_of[:, 0], pairs_of[:, 1])
    sizes = [2 if turn < rest_blocks else 1 for turn in range(handled_blocks)]
    offsets = [0]
    for distance in range(1, reach + 1):
        offsets += [-distance, distance]


    def picked(values, which):
        return jnp.concatenate([values[:, block : block + 1] for block in which], axis=1)

    arranged = jnp.where(
        lon_place == 0,
        picked(spread, [pair[0] for pair in order]),
        picked(spread, [pair[1] for pair in order]),
    )

    def held_by(offset, who):
        index = (group + offset + reach) * 2 + (member if who == 0 else 1 - member)
        return lax.dynamic_index_in_dim(arranged, index, 0, keepdims=False)

    held_of = {(offset, who): held_by(offset, who) for offset in offsets for who in range(2)}
    near = []
    start = 0
    for size in sizes:
        for offset in offsets:
            for who in range(2):
                near.append(held_of[offset, who][start : start + size].reshape(-1))
        start += size
    near = jnp.concatenate(near)
    home = jnp.concatenate([held_of[0, who].reshape(-1) for who in range(2)])

    padded_spectrum = jnp.pad(spectrum, ((0, padded - slots), (0, 0), (0, 0)))

    def to_send(low, high):
        zero_takes = padded_spectrum[block_of[0][low] * ROUND :][: (high - low) * ROUND]
        one_takes = jnp.concatenate(
            [
                padded_spectrum[block * ROUND : (block + 1) * ROUND]
                for block in block_of[1][low:high]
            ]
        )
        chosen = jnp.where(lon_place == 0, one_takes, zero_takes)
        return lax.ppermute(chosen.astype(jnp.bfloat16), "lon", swap)

    terrain = jnp.stack([water_depth, sea_mask.astype(jnp.float32)])
    terrain = jnp.concatenate([terrain, lax.ppermute(terrain, "lon", swap)], axis=2)
    first_other = to_send(0, 1)
    rest_other = to_send(1, handled_blocks) if handled_blocks > 1 else None
    depth, ocean = terrain[0], terrain[1]
    face_x = 0.5 * ocean * jnp.roll(ocean, -1, axis=1)
    face_left = jnp.roll(face_x, 1, axis=1)
    face_y = 0.5 * ocean * jnp.pad(ocean[1:], ((0, 1), (0, 0)))
    fields = [value[:, None] for value in (depth, ocean, face_x, face_left, face_y)]

    own_comps = lax.dynamic_index_in_dim(comps, comp_place, 0, keepdims=False)
    held = jnp.where(
        lon_place == 0,
        picked(own_comps[None], block_of[0])[0],
        picked(own_comps[None], block_of[1])[0],
    )
    real = held >= 0
    held = jnp.where(real, held, 0)
    held_freq = held // NDIR
    wavenumber = (2.0 * math.pi * frequency_of(held_freq)) ** 2 / 9.81
    heading = heading_of(held % NDIR)
    count = jnp.where(real, jnp.take(substeps, held_freq), 0)
    params = jnp.stack(
        [wavenumber, jnp.cos(heading), jnp.sin(heading), count.astype(jnp.float32)], axis=1
    )
    params = jnp.broadcast_to(params[..., None], params.shape + (half,))
    most = jnp.max(count, axis=1)
    both = [(i, j, i ^ 1, 1 - j) for i in range(comp_count) for j in range(2)]
    both = [(i * 2 + j, k * 2 + l) for i, j, k, l in both]

    part_rows = lat // 2
    inputs, homes = [], []
    routes = 1 + 2 * reach
    for turn in range(handled_blocks):
        table = jnp.stack([held_blocks[turn], member]).astype(jnp.int32)
        if turn >= 2:
            first = (turn - 2) * routes
            low = max(first - routes, 0)
            tied = lax.optimization_barrier((table, inputs[low : first + 1]))
            table, inputs[low : first + 1] = tied
        keep, over_lon, over_pair, over_both = advance(
            table,
            most[turn : turn + 1],
            padded_spectrum,
            first_other if turn == 0 else rest_other,
            max(turn - 1, 0),
            fields,
            params[turn],
        )
        if turn < rest_blocks:
            parts = [
                keep,
                lax.ppermute(over_lon, "lon", swap),
                lax.ppermute(over_pair, "comp", pairs),
                lax.ppermute(over_both, ("comp", "lon"), both),
            ]
        else:
            parts = [keep, lax.ppermute(over_pair, "comp", pairs)]
        block = jnp.concatenate(parts, axis=1)
        inputs.append(block)
        homes.append(True)
        for distance in range(1, reach + 1):
            step = 2 * distance
            up = [(i, i + step) for i in range(comp_count - step)]
            down = [(i + step, i) for i in range(comp_count - step)]
            for route in (up, down):
                inputs.append(lax.ppermute(block, "comp", route))
                homes.append(False)

    near, home, inputs[-routes] = lax.optimization_barrier((near, home, inputs[-routes]))
    home_safe = jnp.where(home >= 0, home, 0)
    home_heading = heading_of(home_safe % NDIR)
    home_scale = jnp.sqrt(frequency_of(home_safe // NDIR) / 0.2)
    scales = jnp.stack(
        [
            over_lanes(home_scale * jnp.cos(home_heading), half),
            over_lanes(home_scale * jnp.sin(home_heading), half),
        ]
    )
    directions = jnp.arange(NDIR, dtype=jnp.int32)
    home_dir = (home[:, None] % NDIR == directions[None]).astype(jnp.bfloat16)
    near_dir = (near[:, None] % NDIR == directions[None]).astype(jnp.bfloat16)
    gap = near[None] // NDIR - home[:, None] // NDIR
    matrix = None
    for index in range(5):
        rows = jnp.dot(home_dir, coupling[index], preferred_element_type=jnp.bfloat16)
        term = jnp.dot(rows, near_dir.T, preferred_element_type=jnp.bfloat16)
        term = jnp.where(gap == index - 2, term, jnp.zeros_like(term))
        matrix = term if matrix is None else matrix + term

    wind = lax.dynamic_slice_in_dim(wind_field, member * part_rows, part_rows, axis=1)[:, :, None]
    chunk_rows = part_rows // CHUNKS
    values = [[], []]
    for chunk in range(CHUNKS):
        kept, sent_back = sources(
            matrix, scales, wind, inputs, homes, chunk * chunk_rows, chunk_rows
        )
        values[0].append(kept)
        values[1].append(lax.ppermute(sent_back, "comp", pairs))
    out_table = jnp.concatenate([held_order, member[None]]).astype(jnp.int32)
    return finish(out_table, values[0] + values[1], lat)[:slots]


def solution(mesh):
    in_specs = (
        P(("grp", "comp"), None, "lon"),
        P(None, "lon"),
        P(None, "lon"),
        P(None, "grp", "lon"),
        P(),
        P(),
        P(),
    )
    out_specs = P(("grp", "comp"), None, "lon")
    return jax.shard_map(
        on_device, mesh=mesh, in_specs=in_specs, out_specs=out_specs, check_vma=False
    )
```
